32 devices in a mesh: gx: 4 (over z), gy: 2 (over y), gz: 4 (over x, core).
Axes of the slice: x: 2, y: 2, z: 4, core: 2. Of those that a mesh axis runs over, the one named last changes fastest.
Arguments:
- tokens: bfloat16 [1024, 6144], P('gx', ('gy', 'gz')), may hold values from -6 to 6
- weight_in: bfloat16 [6144, 24576], P('gy', ('gx', 'gz')), may hold values from -0.078125 to 0.078125
- weight_out: bfloat16 [24576, 6144], P(('gx', 'gz'), 'gy'), may hold values from -0.0390625 to 0.0390625
- grad_out: bfloat16 [1024, 6144], P('gx', ('gy', 'gz')), may hold values from -6 to 6
Outputs:
- out: bfloat16 [1024, 6144], P('gx', ('gy', 'gz'))
- grad_tokens: bfloat16 [1024, 6144], P('gx', ('gy', 'gz'))
- grad_weight_in: bfloat16 [6144, 24576], P('gy', ('gx', 'gz'))
- grad_weight_out: bfloat16 [24576, 6144], P(('gx', 'gz'), 'gy')
The draws below stay inside these ranges and needn't reach their ends.
All inputs are finite; a program needn't handle non-finite values.
Results may differ from the reference program's by a relative error of at most 0.025.
Values may be sent and summed in bfloat16 or wider, within the bound.
A program may use at most 192 MiB of HBM per device.

```python
import jax
import jax.numpy as jnp
from jax import lax

D = 6144
FF = 24576
TOK_DEV = 256
TOKENS = 1024
KBLK = 3072


def level_of(rng, shape, pieces, least, top_value):
    def one(axis_at, blocks):
        draws = jax.random.uniform(jax.random.fold_in(jax.random.fold_in(rng, 6), axis_at), (blocks,), jnp.float32, least / len(pieces), top_value / len(pieces))
        return jnp.repeat(jnp.exp(draws), shape[axis_at] // blocks).reshape((-1,) + (1,) * (len(shape) - axis_at - 1))

    loudness = one(*pieces[0])
    for cut in pieces[1:]:
        loudness = loudness * one(*cut)
    return loudness


def gaussian(stream_key, extent, deviation, limit, shards=(), dtype=jnp.bfloat16):
    level = level_of(stream_key, extent, shards, -0.22, 0.18) if shards else 1.0
    values = jax.random.normal(stream_key, extent, jnp.float32) * deviation * level
    return jnp.minimum(jnp.maximum(values, -limit), limit).astype(dtype)


def setup_inputs(seed: int = 0) -> dict:
    splits = jax.random.split(jax.random.key(seed), 5)
    tokens = gaussian(splits[0], (TOKENS, D), 1.0, 6.0, ((0, 4), (1, 8)))
    weight_in = gaussian(splits[1], (D, FF), D ** -0.5, 0.078125, ((0, 2), (1, 16)))
    weight_out = gaussian(splits[2], (FF, D), FF ** -0.5, 0.0390625, ((0, 16), (1, 2)))
    grad_out = gaussian(splits[3], (TOKENS, D), 1.0, 6.0, ((0, 4), (1, 8)))
    return {"tokens": tokens, "weight_in": weight_in, "weight_out": weight_out, "grad_out": grad_out}


half_root = 0.7071067811865476
inv_root_tau = 0.3989422804014327


def gelu_value(preact):
    return 0.5 * preact * (1.0 + jax.scipy.special.erf(preact * half_root))


def gelu_slope(preact):
    return 0.5 * (1.0 + jax.scipy.special.erf(preact * half_root)) + preact * inv_root_tau * jnp.exp(-0.5 * preact * preact)


def rounded(values):
    return lax.optimization_barrier(values.astype(jnp.bfloat16)).astype(jnp.float32)


def width_blocks(left, right_blocks):
    rows = left.shape[0]
    count = right_blocks.shape[0]
    left_blocks = left.reshape(rows, count, KBLK).transpose(1, 0, 2)

    def accumulate(total, paired):
        return total + rounded(jnp.dot(paired[0], paired[1], preferred_element_type=jnp.float32)), None

    start = jnp.zeros((rows, right_blocks.shape[2]), jnp.float32)
    total, unused = lax.scan(accumulate, start, (left_blocks, right_blocks))
    return total


def token_blocks(left, right):
    count = left.shape[0] // TOK_DEV
    left_blocks = left.reshape(count, TOK_DEV, left.shape[1])
    right_blocks = right.reshape(count, TOK_DEV, right.shape[1])

    def accumulate(total, paired):
        product = lax.dot_general(paired[0], paired[1], (((0,), (0,)), ((), ())), preferred_element_type=jnp.float32)
        return total + rounded(product), None

    start = jnp.zeros((left.shape[1], right.shape[1]), jnp.float32)
    total, unused = lax.scan(accumulate, start, (left_blocks, right_blocks))
    return total


def reference(tokens, weight_in, weight_out, grad_out):
    count = D // KBLK
    preact = width_blocks(tokens, weight_in.reshape(count, KBLK, FF))
    active = gelu_value(preact).astype(jnp.bfloat16)
    out = jnp.dot(active, weight_out, preferred_element_type=jnp.float32).astype(jnp.bfloat16)
    grad_active = width_blocks(grad_out, weight_out.reshape(FF, count, KBLK).transpose(1, 2, 0))
    grad_preact = (grad_active * gelu_slope(preact)).astype(jnp.bfloat16)
    grad_weight_out = token_blocks(active, grad_out).astype(jnp.bfloat16)
    grad_weight_in = token_blocks(tokens, grad_preact).astype(jnp.bfloat16)
    grad_tokens = lax.dot_general(grad_preact, weight_in, (((1,), (1,)), ((), ())), preferred_element_type=jnp.float32).astype(jnp.bfloat16)
    return out, grad_tokens, grad_weight_in, grad_weight_out
```

```python
import jax
import jax.numpy as jnp
from jax import lax
from jax.sharding import PartitionSpec as P

half_root = 0.7071067811865476
inv_root_tau = 0.3989422804014327
pieces = 2


def gelu_value(preact):
    return 0.5 * preact * (1.0 + jax.scipy.special.erf(preact * half_root))


def gelu_slope(preact):
    return 0.5 * (
        1.0 + jax.scipy.special.erf(preact * half_root)
    ) + preact * inv_root_tau * jnp.exp(-0.5 * preact * preact)


def contract_rows(left, right):
    return lax.dot_general(
        left, right, (((0,), (0,)), ((), ())), preferred_element_type=jnp.float32
    )


def contract_cols(left, right):
    return lax.dot_general(
        left, right, (((1,), (1,)), ((), ())), preferred_element_type=jnp.float32
    )


def split_rows(values):
    rows = values.shape[0] // pieces
    return [values[at * rows : (at + 1) * rows] for at in range(pieces)]


def gather_tokens(part):
    part = lax.all_gather(part, "gx", axis=0, tiled=True)
    return lax.all_gather(part, "gz", axis=1, tiled=True)


def exchange(partial, width):
    return [
        lax.ppermute(partial, "gy", [(at, (at + shift) % width) for at in range(width)])
        for shift in range(1, width)
    ]


def add_blocks(own, others):
    total = own.astype(jnp.float32)
    for other in others:
        total = total + other.astype(jnp.float32)
    return total


def scatter_terms(terms):
    terms = lax.psum_scatter(
        terms.astype(jnp.bfloat16), "gz", scatter_dimension=1, tiled=True
    )
    return lax.psum_scatter(terms, "gx", scatter_dimension=0, tiled=True)


def solution(mesh):
    width = mesh.shape["gy"]

    def per_device(tokens, weight_in, weight_out, grad_out):
        features = [gather_tokens(part) for part in split_rows(tokens)]
        grad_feats = [gather_tokens(part) for part in split_rows(grad_out)]
        own_pre = [
            jnp.dot(part, weight_in, preferred_element_type=jnp.float32).astype(jnp.bfloat16)
            for part in features
        ]
        far_pre = [exchange(part, width) for part in own_pre]
        own_grad = [
            contract_cols(part, weight_out).astype(jnp.bfloat16) for part in grad_feats
        ]
        far_grad = [exchange(part, width) for part in own_grad]
        preact = [add_blocks(own, far) for own, far in zip(own_pre, far_pre)]
        active = [gelu_value(part).astype(jnp.bfloat16) for part in preact]
        out = [
            scatter_terms(jnp.dot(part, weight_out, preferred_element_type=jnp.float32))
            for part in active
        ]
        grad_preact = [
            (add_blocks(own, far) * gelu_slope(pre)).astype(jnp.bfloat16)
            for own, far, pre in zip(own_grad, far_grad, preact)
        ]
        grad_tokens = [
            scatter_terms(contract_cols(part, weight_in)) for part in grad_preact
        ]
        grad_weight_out = contract_rows(
            jnp.concatenate(active), jnp.concatenate(grad_feats)
        ).astype(jnp.bfloat16)
        grad_weight_in = contract_rows(
            jnp.concatenate(features), jnp.concatenate(grad_preact)
        ).astype(jnp.bfloat16)
        return (
            jnp.concatenate(out),
            jnp.concatenate(grad_tokens),
            grad_weight_in,
            grad_weight_out,
        )

    return jax.shard_map(
        per_device,
        mesh=mesh,
        in_specs=(
            P("gx", ("gy", "gz")),
            P("gy", ("gx", "gz")),
            P(("gx", "gz"), "gy"),
            P("gx", ("gy", "gz")),
        ),
        out_specs=(
            P("gx", ("gy", "gz")),
            P("gx", ("gy", "gz")),
            P("gy", ("gx", "gz")),
            P(("gx", "gz"), "gy"),
        ),
        check_vma=False,
    )
```

```python
import jax
import jax.numpy as jnp
from jax import lax
from jax.sharding import PartitionSpec as P

half_root = 0.7071067811865476
inv_root_tau = 0.3989422804014327
pieces = 2


def gelu_value(preact):
    return 0.5 * preact * (1.0 + jax.scipy.special.erf(preact * half_root))


def gelu_slope(preact):
    return 0.5 * (
        1.0 + jax.scipy.special.erf(preact * half_root)
    ) + preact * inv_root_tau * jnp.exp(-0.5 * preact * preact)


def contract_rows(left, right):
    return lax.dot_general(
        left, right, (((0,), (0,)), ((), ())), preferred_element_type=jnp.float32
    )


def contract_cols(left, right):
    return lax.dot_general(
        left, right, (((1,), (1,)), ((), ())), preferred_element_type=jnp.float32
    )


def split_rows(values):
    rows = values.shape[0] // pieces
    return [values[at * rows : (at + 1) * rows] for at in range(pieces)]


def gather_rows(part, count):
    rest = [
        lax.ppermute(part, "gx", [(at, (at + shift) % count) for at in range(count)])
        for shift in range(1, count)
    ]
    return jnp.concatenate([part] + rest)


def gather_in_turn(parts, count):
    gathered = []
    for part in parts:
        if gathered:
            part, gathered[-1] = lax.optimization_barrier((part, gathered[-1]))
        gathered.append(gather_rows(part, count))
    return [lax.all_gather(part, "gz", axis=1, tiled=True) for part in gathered]


def exchange(partial, width):
    return [
        lax.ppermute(partial, "gy", [(at, (at + shift) % width) for at in range(width)])
        for shift in range(1, width)
    ]


def add_blocks(own, others):
    total = own.astype(jnp.float32)
    for other in others:
        total = total + other.astype(jnp.float32)
    return total


def scatter_near(terms, count):
    if count != 4:
        return lax.psum_scatter(terms, "gz", scatter_dimension=1, tiled=True)
    low = lax.axis_index("gz") % 2
    block = terms.shape[1] // count

    def columns(at):
        return lax.dynamic_slice_in_dim(terms, at * block, block, axis=1)

    near = jnp.stack([columns(1 - low), columns(3 - low)])
    near = lax.ppermute(near, "gz", [(at, at ^ 1) for at in range(count)])
    own = jnp.stack([columns(low), columns(2 + low)])
    return (own.astype(jnp.float32) + near.astype(jnp.float32)).astype(jnp.bfloat16)


def scatter_far(total, count):
    if count != 4:
        return total
    high = lax.axis_index("gz") // 2
    far = lax.dynamic_index_in_dim(total, 1 - high, 0, keepdims=False)
    far = lax.ppermute(far, "gz", [(at, at ^ 2) for at in range(count)])
    kept = lax.dynamic_index_in_dim(total, high, 0, keepdims=False)
    return (kept.astype(jnp.float32) + far.astype(jnp.float32)).astype(jnp.bfloat16)


def scatter_rows(terms, count):
    rows = terms.shape[0] // count
    total = terms[:rows].astype(jnp.float32)
    for shift in range(1, count):
        far = lax.ppermute(
            terms[shift * rows : (shift + 1) * rows],
            "gx",
            [(at, (at - shift) % count) for at in range(count)],
        )
        total = total + far.astype(jnp.float32)
    return total.astype(jnp.bfloat16)


def solution(mesh):
    width, deep, wide = mesh.shape["gy"], mesh.shape["gx"], mesh.shape["gz"]

    def per_device(tokens, weight_in, weight_out, grad_out):
        gathered = gather_in_turn(split_rows(tokens) + split_rows(grad_out), deep)
        features, grad_feats = gathered[:pieces], gathered[pieces:]
        own_pre = [
            jnp.dot(part, weight_in, preferred_element_type=jnp.float32).astype(jnp.bfloat16)
            for part in features
        ]
        far_pre = [exchange(part, width) for part in own_pre]
        own_grad = [
            contract_cols(part, weight_out).astype(jnp.bfloat16) for part in grad_feats
        ]
        far_grad = [exchange(part, width) for part in own_grad]
        preact = [add_blocks(own, far) for own, far in zip(own_pre, far_pre)]
        active = [gelu_value(part).astype(jnp.bfloat16) for part in preact]
        out_near = [
            scatter_near(
                jnp.dot(part, weight_out, preferred_element_type=jnp.float32).astype(jnp.bfloat16),
                wide,
            )
            for part in active
        ]
        grad_weight_out = contract_rows(
            jnp.concatenate(active), jnp.concatenate(grad_feats)
        ).astype(jnp.bfloat16)
        out_far, grad_preact, grad_near = [], [], []
        for at in range(pieces):
            far, pre_far = far_grad[at], far_pre[at]
            if at == 0:
                out_near, far, pre_far = lax.optimization_barrier((out_near, far, pre_far))
                out_far = [scatter_far(part, wide) for part in out_near]
            elif at == pieces - 1:
                unused, out_far, grad_near, far, pre_far = lax.optimization_barrier(
                    (grad_weight_out[:8, :128], out_far, grad_near, far, pre_far)
                )
                out = [scatter_rows(part, deep) for part in out_far]
            slope = gelu_slope(add_blocks(own_pre[at], pre_far))
            grad_preact.append((add_blocks(own_grad[at], far) * slope).astype(jnp.bfloat16))
            terms = contract_cols(grad_preact[at], weight_in).astype(jnp.bfloat16)
            grad_near.append(scatter_near(terms, wide))
        grad_tokens = [scatter_rows(scatter_far(part, wide), deep) for part in grad_near]
        grad_weight_in = contract_rows(
            jnp.concatenate(features), jnp.concatenate(grad_preact)
        ).astype(jnp.bfloat16)
        return (
            jnp.concatenate(out),
            jnp.concatenate(grad_tokens),
            grad_weight_in,
            grad_weight_out,
        )

    return jax.shard_map(
        per_device,
        mesh=mesh,
        in_specs=(
            P("gx", ("gy", "gz")),
            P("gy", ("gx", "gz")),
            P(("gx", "gz"), "gy"),
            P("gx", ("gy", "gz")),
        ),
        out_specs=(
            P("gx", ("gy", "gz")),
            P("gx", ("gy", "gz")),
            P("gy", ("gx", "gz")),
            P(("gx", "gz"), "gy"),
        ),
        check_vma=False,
    )
```

```python
import jax
import jax.numpy as jnp
from jax import lax
from jax.sharding import PartitionSpec as P

half_root = 0.7071067811865476
inv_root_tau = 0.3989422804014327
pieces = 2


def gelu_value(preact):
    return 0.5 * preact * (1.0 + jax.scipy.special.erf(preact * half_root))


def gelu_slope(preact):
    return 0.5 * (
        1.0 + jax.scipy.special.erf(preact * half_root)
    ) + preact * inv_root_tau * jnp.exp(-0.5 * preact * preact)


def contract_rows(left, right):
    return lax.dot_general(
        left, right, (((0,), (0,)), ((), ())), preferred_element_type=jnp.float32
    )


def contract_cols(left, right):
    return lax.dot_general(
        left, right, (((1,), (1,)), ((), ())), preferred_element_type=jnp.float32
    )


def split_rows(values):
    rows = values.shape[0] // pieces
    return [values[at * rows : (at + 1) * rows] for at in range(pieces)]


def gather_rows(part, count):
    rest = [
        lax.ppermute(part, "gx", [(at, (at + shift) % count) for at in range(count)])
        for shift in range(1, count)
    ]
    return jnp.concatenate([part] + rest)


def after(value, *earlier):
    return lax.optimization_barrier((value,) + earlier)[0]


def exchange(partial, width):
    return [
        lax.ppermute(partial, "gy", [(at, (at + shift) % width) for at in range(width)])
        for shift in range(1, width)
    ]


def add_blocks(own, others):
    total = own.astype(jnp.float32)
    for other in others:
        total = total + other.astype(jnp.float32)
    return total


def scatter_near(terms, count):
    if count != 4:
        return lax.psum_scatter(terms, "gz", scatter_dimension=1, tiled=True)
    low = lax.axis_index("gz") % 2
    block = terms.shape[1] // count

    def columns(at):
        return lax.dynamic_slice_in_dim(terms, at * block, block, axis=1)

    near = jnp.stack([columns(1 - low), columns(3 - low)])
    near = lax.ppermute(near, "gz", [(at, at ^ 1) for at in range(count)])
    own = jnp.stack([columns(low), columns(2 + low)])
    return (own.astype(jnp.float32) + near.astype(jnp.float32)).astype(jnp.bfloat16)


def scatter_far(total, count):
    if count != 4:
        return total
    high = lax.axis_index("gz") // 2
    far = lax.dynamic_index_in_dim(total, 1 - high, 0, keepdims=False)
    far = lax.ppermute(far, "gz", [(at, at ^ 2) for at in range(count)])
    kept = lax.dynamic_index_in_dim(total, high, 0, keepdims=False)
    return (kept.astype(jnp.float32) + far.astype(jnp.float32)).astype(jnp.bfloat16)


def scatter_rows(terms, count):
    rows = terms.shape[0] // count
    total = terms[:rows].astype(jnp.float32)
    for shift in range(1, count):
        far = lax.ppermute(
            terms[shift * rows : (shift + 1) * rows],
            "gx",
            [(at, (at - shift) % count) for at in range(count)],
        )
        total = total + far.astype(jnp.float32)
    return total.astype(jnp.bfloat16)


def solution(mesh):
    width, deep, wide = mesh.shape["gy"], mesh.shape["gx"], mesh.shape["gz"]

    def per_device(tokens, weight_in, weight_out, grad_out):
        def project(part):
            product = jnp.dot(part, weight_in, preferred_element_type=jnp.float32)
            return product.astype(jnp.bfloat16)

        parts = split_rows(tokens) + split_rows(grad_out)
        rows, gathered, own_pre = None, [], []
        for at, part in enumerate(parts):
            if at:
                part, rows = lax.optimization_barrier((part, rows))
                gathered.append(lax.all_gather(rows, "gz", axis=1, tiled=True))
            if at >= pieces:
                own_pre.append(project(gathered[at - pieces]))
                part = after(part, own_pre[-1])
            rows = gather_rows(part, deep)
        gathered.append(lax.all_gather(rows, "gz", axis=1, tiled=True))
        features, grad_feats = gathered[:pieces], gathered[pieces:]
        far_pre = [exchange(part, width) for part in own_pre]
        own_grad = jnp.concatenate(
            [contract_cols(part, weight_out).astype(jnp.bfloat16) for part in grad_feats]
        )
        own_grad, far_pre[1:] = lax.optimization_barrier((own_grad, far_pre[1:]))
        far_grad = exchange(own_grad, width)
        own_grad = split_rows(own_grad)
        preact = [add_blocks(own, far) for own, far in zip(own_pre, far_pre)]
        active = [gelu_value(part).astype(jnp.bfloat16) for part in preact]
        out_near = [
            scatter_near(
                jnp.dot(part, weight_out, preferred_element_type=jnp.float32).astype(jnp.bfloat16),
                wide,
            )
            for part in active
        ]
        out_far = [scatter_far(part, wide) for part in out_near]
        out_far, far_grad, far_pre = lax.optimization_barrier((out_far, far_grad, far_pre))
        far_grad = list(zip(*[split_rows(part) for part in far_grad]))
        grad_preact, grad_near = [], []
        for at in range(pieces):
            far, pre_far = far_grad[at], far_pre[at]
            slope = gelu_slope(add_blocks(own_pre[at], pre_far))
            grad_preact.append((add_blocks(own_grad[at], far) * slope).astype(jnp.bfloat16))
            terms = contract_cols(grad_preact[at], weight_in).astype(jnp.bfloat16)
            grad_near.append(scatter_near(terms, wide))
        out = [scatter_rows(part, deep) for part in out_far]
        grad_far = [scatter_far(part, wide) for part in grad_near[:-1]]
        grad_near[-1], grad_far, last, last_active = lax.optimization_barrier(
            (grad_near[-1], grad_far, grad_preact[-1], active[-1])
        )
        grad_far.append(scatter_far(grad_near[-1], wide))
        grad_tokens = [scatter_rows(part, deep) for part in grad_far]
        grad_weight_in = contract_rows(
            jnp.concatenate(features), jnp.concatenate(grad_preact[:-1] + [last])
        ).astype(jnp.bfloat16)
        grad_weight_out = contract_rows(
            jnp.concatenate(active[:-1] + [last_active]), jnp.concatenate(grad_feats)
        ).astype(jnp.bfloat16)
        return (
            jnp.concatenate(out),
            jnp.concatenate(grad_tokens),
            grad_weight_in,
            grad_weight_out,
        )

    return jax.shard_map(
        per_device,
        mesh=mesh,
        in_specs=(
            P("gx", ("gy", "gz")),
            P("gy", ("gx", "gz")),
            P(("gx", "gz"), "gy"),
            P("gx", ("gy", "gz")),
        ),
        out_specs=(
            P("gx", ("gy", "gz")),
            P("gx", ("gy", "gz")),
            P("gy", ("gx", "gz")),
            P(("gx", "gz"), "gy"),
        ),
        check_vma=False,
    )
```
